32 devices in a mesh: seq: 8 (over z, x), head: 4 (over y, core).
Axes of the slice: x: 2, y: 2, z: 4, core: 2. Of those that a mesh axis runs over, the one named last changes fastest.
Arguments:
- queries: bfloat16 [1024, 4096], P('seq', 'head'), may hold values from -150 to 150
- neighbours: bfloat16 [8, 128, 8, 448], P(None, 'seq', None, 'head'), may hold values from -6 to 6
- key_weight: bfloat16 [448, 4096], P(None, 'head'), may hold values from -0.25 to 0.25
- value_weight: bfloat16 [448, 4096], P(None, 'head'), may hold values from -0.25 to 0.25
- counts: int32 [16], P('seq'), may hold values from 1 to 4, as said below
- slot_map: int32 [8, 8], P('seq'), may hold values from 0 to 7, each once within a row
- d_attended: bfloat16 [1024, 4096], P('seq', 'head'), may hold values from -6 to 6
Outputs:
- attended: bfloat16 [1024, 4096], P('seq', 'head')
- d_queries: bfloat16 [1024, 4096], P('seq', 'head')
- d_neighbours: bfloat16 [8, 128, 8, 448], P(None, 'seq', None, 'head')
The draws below stay inside these ranges and needn't reach their ends.
Inputs may be any that keep to these rules, and one draw needn't show every extreme that they name: `counts`: every span has at least one neighbour; some span has 4. `slot_map`: each row is a permutation; entry c * 4 + j names the slot that holds neighbour j of local span c, and only entries with j below the span's count are used.
All inputs are finite; a program needn't handle non-finite values.
Results may differ from the reference program's by a relative error of at most 0.03.
Values may be sent and summed in bfloat16 or wider, within the bound.
A program may use at most 64 MiB of HBM per device.

```python
import jax
import jax.numpy as jnp
from jax import lax

HEADS = 32
HDIM = 128
ENC = 448
SPAN = 64
NB_LEN = 128
MAX_NB = 4
CH_DEV = 2
TOK_DEV = 128
SLOTS = 8
TOKENS = 1024
SPANS = 16
GROUPS = 8
N_SEQ = 8
N_HEAD = 4


def draw_queries(key, part):
    shape = (TOKENS, HEADS * HDIM)
    values = jnp.clip(jax.random.normal(jax.random.fold_in(key, 4), shape, jnp.float32), -6.0, 6.0)
    return values.astype(jnp.bfloat16)


def draw_counts(key, part):
    values = jax.random.randint(jax.random.fold_in(key, 11), (SPANS,), 1, MAX_NB + 1)
    spot = jax.random.randint(jax.random.fold_in(key, 12), (), 0, SPANS)
    values = values.at[spot].set(MAX_NB)
    return values.astype(jnp.int32)


def steps_of(stream_key, shape, pieces, low, high):
    def one(dim, blocks):
        heights = jax.random.uniform(jax.random.fold_in(jax.random.fold_in(stream_key, 6), dim), (blocks,), jnp.float32, low / len(pieces), high / len(pieces))
        return jnp.repeat(jnp.exp(heights), shape[dim] // blocks).reshape((-1,) + (1,) * (len(shape) - dim - 1))

    loudness = one(*pieces[0])
    for cut in pieces[1:]:
        loudness = loudness * one(*cut)
    return loudness


def noise(key, shape, deviation, reach, split=(), kind=jnp.bfloat16):
    array = jax.random.normal(key, shape, jnp.float32) * deviation
    if len(split) > 0:
        array = steps_of(key, shape, split, -0.22, 0.18) * array
    return jnp.clip(array, min=-reach, max=reach).astype(kind)


def setup_inputs(seed: int = 0) -> dict:
    streams_of = jax.random.split(jax.random.key(seed), 8)
    return {
        "queries": draw_queries(jax.random.fold_in(streams_of[7], 71), 0),
        "neighbours": noise(streams_of[1], (GROUPS, NB_LEN, SLOTS, ENC), 1.0, 6.0, ((1, 8), (3, 4))),
        "key_weight": noise(streams_of[2], (ENC, HEADS * HDIM), ENC ** -0.5, 0.25, ((1, 4),)),
        "value_weight": noise(streams_of[3], (ENC, HEADS * HDIM), ENC ** -0.5, 0.25, ((1, 4),)),
        "counts": draw_counts(jax.random.fold_in(streams_of[7], 71), 0),
        "slot_map": jax.vmap(lambda own: jax.random.permutation(own, SLOTS))(jax.random.split(streams_of[5], GROUPS)).reshape((GROUPS, SLOTS)).astype(jnp.int32),
        "d_attended": noise(streams_of[6], (TOKENS, HEADS * HDIM), 1.0, 6.0, ((0, 8), (1, 4))),
    }


def present_table(count_row, slot_row):
    chosen = slot_row.reshape(CH_DEV, MAX_NB)
    ranks = jnp.arange(MAX_NB, dtype=jnp.int32)
    valid = ranks[None, :] < count_row[:, None]
    slot_ids = jnp.arange(SLOTS, dtype=jnp.int32)
    hits = valid[:, :, None] & (chosen[:, :, None] == slot_ids[None, None, :])
    return jnp.any(hits, axis=1)


def attend_group(query_rows, enc_rows, count_row, slot_row, grad_rows, key_weight, value_weight):
    total_rows = NB_LEN * SLOTS
    width = HEADS * HDIM
    highest = lax.Precision.HIGHEST
    flat_rows = enc_rows.reshape(total_rows, ENC)
    keys = jnp.dot(flat_rows, key_weight, preferred_element_type=jnp.float32)
    values = jnp.dot(flat_rows, value_weight, preferred_element_type=jnp.float32).astype(jnp.bfloat16)
    present = present_table(count_row, slot_row)
    allowed = jnp.tile(jnp.repeat(present, SPAN, axis=0), (1, NB_LEN))
    factor = 1.0 / (HDIM ** 0.5)
    query_heads = query_rows.reshape(TOK_DEV, HEADS, HDIM).astype(jnp.float32)
    key_heads = keys.reshape(total_rows, HEADS, HDIM).astype(jnp.float32)
    value_heads = values.reshape(total_rows, HEADS, HDIM).astype(jnp.float32)
    grad_heads = grad_rows.reshape(TOK_DEV, HEADS, HDIM).astype(jnp.float32)
    scores = jnp.einsum("thd,rhd->htr", query_heads, key_heads, precision=highest) * factor
    scores = jnp.where(allowed[None, :, :], scores, -jnp.inf)
    top = jnp.max(scores, axis=-1, keepdims=True)
    expo = jnp.exp(scores - top)
    probs = expo / jnp.sum(expo, axis=-1, keepdims=True)
    probs_b = probs.astype(jnp.bfloat16)
    attended = jnp.einsum("htr,rhd->thd", probs_b.astype(jnp.float32), value_heads)
    attended = attended.astype(jnp.bfloat16).reshape(TOK_DEV, width)
    dprobs = jnp.einsum("thd,rhd->htr", grad_heads, value_heads)
    inner = jnp.sum(probs * dprobs, axis=-1, keepdims=True)
    dscores = (probs * (dprobs - inner)).astype(jnp.bfloat16).astype(jnp.float32)
    d_queries = (jnp.einsum("htr,rhd->thd", dscores, key_heads, precision=highest) * factor).astype(jnp.bfloat16)
    d_keys = (jnp.einsum("htr,thd->rhd", dscores, query_heads) * factor).astype(jnp.bfloat16)
    d_values = jnp.einsum("htr,thd->rhd", probs_b.astype(jnp.float32), grad_heads).astype(jnp.bfloat16)
    local_width = width // N_HEAD
    dk_blocks = d_keys.reshape(total_rows, N_HEAD, local_width).astype(jnp.float32)
    dv_blocks = d_values.reshape(total_rows, N_HEAD, local_width).astype(jnp.float32)
    wk_blocks = key_weight.reshape(ENC, N_HEAD, local_width).astype(jnp.float32)
    wv_blocks = value_weight.reshape(ENC, N_HEAD, local_width).astype(jnp.float32)
    partial_value = jnp.einsum("rjc,ejc->jre", dk_blocks, wk_blocks) + jnp.einsum("rjc,ejc->jre", dv_blocks, wv_blocks)
    partial_value = lax.optimization_barrier(partial_value.astype(jnp.bfloat16)).astype(jnp.float32)
    summed = jnp.sum(partial_value, axis=0).astype(jnp.bfloat16).reshape(NB_LEN, SLOTS, ENC)
    return attended, d_queries.reshape(TOK_DEV, width), summed


def reference(queries, neighbours, key_weight, value_weight, counts, slot_map, d_attended):
    width = HEADS * HDIM
    query_groups = queries.reshape(N_SEQ, TOK_DEV, width)
    grad_groups = d_attended.reshape(N_SEQ, TOK_DEV, width)
    count_groups = counts.reshape(N_SEQ, CH_DEV)

    def one_group(items):
        return attend_group(items[0], items[1], items[2], items[3], items[4], key_weight, value_weight)

    attended, d_queries, d_neighbours = lax.map(one_group, (query_groups, neighbours, count_groups, slot_map, grad_groups))
    return attended.reshape(TOKENS, width), d_queries.reshape(TOKENS, width), d_neighbours
```

```python
import functools
import math

import jax
import jax.numpy as jnp
from jax import lax
from jax.experimental import pallas as pl
from jax.experimental.pallas import tpu as pltpu
from jax.sharding import PartitionSpec as P

HDIM = 128
SPAN = 64
NB_LEN = 128
MAX_NB = 4
CH_DEV = 2
SLOTS = 8
LANES = 128
CORES = 2
MESH_ID = pl.DeviceIdType.MESH
VMEM = pltpu.VMEM


def present_table(count_row, slot_row):
    chosen = slot_row.reshape(CH_DEV, MAX_NB)
    ranks = jnp.arange(MAX_NB, dtype=jnp.int32)
    valid = ranks[None, :] < count_row[:, None]
    slot_ids = jnp.arange(SLOTS, dtype=jnp.int32)
    hits = valid[:, :, None] & (chosen[:, :, None] == slot_ids[None, None, :])
    return jnp.any(hits, axis=1)


def per_device_plain(queries, neighbours, key_weight, value_weight, counts, slot_map, d_attended):
    total_rows = NB_LEN * SLOTS
    enc_local = neighbours.shape[3]
    width_local = key_weight.shape[1]
    heads_local = width_local // HDIM
    token_count = queries.shape[0]
    highest = lax.Precision.HIGHEST
    arrived = lax.all_to_all(neighbours, "seq", split_axis=0, concat_axis=1, tiled=True)
    flat_rows = arrived.reshape(total_rows, enc_local)
    portion = lax.all_gather(flat_rows, "head", axis=1, tiled=True)
    key_sum = jnp.dot(portion, key_weight, preferred_element_type=jnp.float32)
    value_sum = jnp.dot(portion, value_weight, preferred_element_type=jnp.float32)
    keys = key_sum.reshape(total_rows, heads_local, HDIM)
    values = value_sum.astype(jnp.bfloat16).reshape(total_rows, heads_local, HDIM)
    present = present_table(counts, slot_map[0])
    allowed = jnp.tile(jnp.repeat(present, SPAN, axis=0), (1, NB_LEN))
    factor = 1.0 / HDIM**0.5
    query_heads = queries.reshape(token_count, heads_local, HDIM)
    grad_heads = d_attended.reshape(token_count, heads_local, HDIM)
    scores = (
        jnp.einsum(
            "thd,rhd->htr",
            query_heads.astype(jnp.float32),
            keys,
            precision=highest,
            preferred_element_type=jnp.float32,
        )
        * factor
    )
    scores = jnp.where(allowed[None, :, :], scores, -jnp.inf)
    top = jnp.max(scores, axis=-1, keepdims=True)
    expo = jnp.exp(scores - top)
    probs = expo / jnp.sum(expo, axis=-1, keepdims=True)
    probs_b = probs.astype(jnp.bfloat16)
    attended = jnp.einsum("htr,rhd->thd", probs_b, values, preferred_element_type=jnp.float32)
    attended = attended.astype(jnp.bfloat16).reshape(token_count, width_local)
    dprobs = jnp.einsum("thd,rhd->htr", grad_heads, values, preferred_element_type=jnp.float32)
    inner = jnp.sum(probs * dprobs, axis=-1, keepdims=True)
    dscores = (probs * (dprobs - inner)).astype(jnp.bfloat16)
    d_queries = (
        jnp.einsum(
            "htr,rhd->thd",
            dscores.astype(jnp.float32),
            keys,
            precision=highest,
            preferred_element_type=jnp.float32,
        )
        * factor
    )
    d_queries = d_queries.astype(jnp.bfloat16).reshape(token_count, width_local)
    d_keys = (
        jnp.einsum("htr,thd->rhd", dscores, query_heads, preferred_element_type=jnp.float32)
        * factor
    )
    d_keys = d_keys.astype(jnp.bfloat16).reshape(total_rows, width_local)
    d_values = jnp.einsum("htr,thd->rhd", probs_b, grad_heads, preferred_element_type=jnp.float32)
    d_values = d_values.astype(jnp.bfloat16).reshape(total_rows, width_local)
    contract = (((1,), (1,)), ((), ()))
    partial_value = lax.dot_general(
        d_keys, key_weight, contract, preferred_element_type=jnp.float32
    )
    partial_value = partial_value + lax.dot_general(
        d_values, value_weight, contract, preferred_element_type=jnp.float32
    )
    summed = lax.psum(partial_value.astype(jnp.bfloat16), "head").astype(jnp.float32)
    own_part = lax.dynamic_slice_in_dim(summed, lax.axis_index("head") * enc_local, enc_local, 1)
    grad_rows = own_part.astype(jnp.bfloat16).reshape(1, NB_LEN, SLOTS, enc_local)
    d_neighbours = lax.all_to_all(grad_rows, "seq", split_axis=1, concat_axis=0, tiled=True)
    return (attended, d_queries, d_neighbours)


def positions(n_seq):
    me = lax.axis_index("seq")
    head = lax.axis_index("head")
    y = head // CORES
    core = head % CORES
    across = (1 - y) * CORES + core
    beside = y * CORES + (1 - core)
    return me, head, y, core, across, beside


def greet(n_seq, me, head, across, beside):
    barrier = pltpu.get_barrier_semaphore()
    for k in range(1, n_seq):
        pl.semaphore_signal(
            barrier, inc=1, device_id=((me + k) % n_seq, head), device_id_type=MESH_ID
        )
    for peer in (across, beside):
        pl.semaphore_signal(barrier, inc=1, device_id=(me, peer), device_id_type=MESH_ID)
    pl.semaphore_wait(barrier, n_seq + 1)


def gather_kernel(n_seq, block, nb_ref, rows_ref, packed, own_sem, s_send, s_recv, y_send, y_recv, c_send, c_recv, f_send, f_recv):
    me, head, y, core, across, beside = positions(n_seq)
    enc_local = nb_ref.shape[1]
    packed[...] = jnp.zeros_like(packed)
    packed[:, :enc_local] = nb_ref[...]
    greet(n_seq, me, head, across, beside)

    def rows_of(quarter, owner):
        return rows_ref.at[quarter, pl.ds(pl.multiple_of(owner * block, block), block), :]

    def remote(src, dst, send, recv, device):
        return pltpu.make_async_remote_copy(
            src_ref=src,
            dst_ref=dst,
            send_sem=send,
            recv_sem=recv,
            device_id=device,
            device_id_type=MESH_ID,
        )

    own = pltpu.make_async_copy(
        packed.at[pl.ds(pl.multiple_of(me * block, block), block), :], rows_of(head, me), own_sem
    )
    own.start()
    sent = []
    for k in range(n_seq - 1, 0, -1):
        to = (me + k) % n_seq
        copy = remote(
            packed.at[pl.ds(pl.multiple_of(to * block, block), block), :],
            rows_of(head, me),
            s_send.at[k],
            s_recv.at[k],
            (to, head),
        )
        copy.start()
        sent.append((k, copy))
    pending = []
    order = [0] + [k for k, _ in sent]
    arrivals = dict(sent)
    own.wait()
    for k in order:
        owner = (me + n_seq - k) % n_seq
        if k > 0:
            arrivals[k].wait_recv()
        over = remote(rows_of(head, owner), rows_of(head, owner), y_send.at[k], y_recv.at[k], (me, across))
        over.start()
        side = remote(rows_of(head, owner), rows_of(head, owner), c_send.at[k], c_recv.at[k], (me, beside))
        side.start()
        pending.append((owner, k, over, side))
    forwards = []
    for owner, k, over, side in pending:
        over.wait_recv()
        forward = remote(
            rows_of(across, owner), rows_of(across, owner), f_send.at[k], f_recv.at[k], (me, beside)
        )
        forward.start()
        forwards.append(forward)
    for owner, k, over, side in pending:
        side.wait_recv()
    for forward in forwards:
        forward.wait_recv()
    for k, copy in sent:
        copy.wait_send()
    for owner, k, over, side in pending:
        over.wait_send()
        side.wait_send()
    for forward in forwards:
        forward.wait_send()


def gather(n_seq, block, rows):
    dma = pltpu.SemaphoreType.DMA
    return pl.pallas_call(
        functools.partial(gather_kernel, n_seq, block),
        out_shape=jax.ShapeDtypeStruct((4, n_seq * block, LANES), jnp.bfloat16),
        in_specs=[pl.BlockSpec(memory_space=VMEM)],
        out_specs=pl.BlockSpec(memory_space=VMEM),
        scratch_shapes=[pltpu.VMEM((n_seq * block, LANES), jnp.bfloat16), dma]
        + [dma((n_seq,)) for _ in range(8)],
        compiler_params=pltpu.CompilerParams(
            collective_id=0, has_side_effects=True, vmem_limit_bytes=16 * 2**20
        ),
        name="gather_rows",
    )(rows)


def dot(a, b, left, right):
    return lax.dot_general(
        a, b, (((left,), (right,)), ((), ())), preferred_element_type=jnp.float32
    )


def padded(weight, enc_local):
    gap = jnp.zeros((LANES - enc_local, weight.shape[1]), weight.dtype)
    parts = []
    for quarter in range(4):
        parts += [weight[quarter * enc_local : (quarter + 1) * enc_local], gap]
    return jnp.concatenate(parts, axis=0)


def attend_kernel(group, counts_ref, slots_ref, rows_ref, q_ref, g_ref, wk_ref, wv_ref, att_ref, dq_ref, part_ref, grads, weights):
    step = pl.program_id(0)
    steps = pl.num_programs(0)
    total_rows = rows_ref.shape[1]
    enc_local = wk_ref.shape[0] // 4
    tokens = q_ref.shape[0]
    factor = 1.0 / HDIM**0.5
    slot = lax.broadcasted_iota(jnp.int32, (SLOTS, tokens), 0)
    span = lax.broadcasted_iota(jnp.int32, (SLOTS, tokens), 1) // SPAN
    bias = jnp.full((SLOTS, tokens), -jnp.inf, jnp.float32)
    for c in range(CH_DEV):
        for j in range(MAX_NB):
            wanted = jnp.where(j < counts_ref[c], slots_ref[0, c * MAX_NB + j], -1)
            bias = jnp.where((slot == wanted) & (span == c), 0.0, bias)
    rows = jnp.concatenate([rows_ref[quarter] for quarter in range(4)], axis=1)
    blank = jnp.zeros((tokens, HDIM), jnp.bfloat16)
    for i in range(group):
        cut = slice(i * HDIM, (i + 1) * HDIM)
        weight = padded(
            jnp.concatenate([wk_ref[:, cut], wv_ref[:, cut]], axis=1), enc_local
        )
        weights[step * group + i] = weight
        both = dot(rows, weight, 1, 0)
        keys = both[:, :HDIM]
        keys_high = keys.astype(jnp.bfloat16)
        keys_low = (keys - keys_high.astype(jnp.float32)).astype(jnp.bfloat16)
        split = jnp.concatenate([keys_high, keys_low], axis=1)
        values = both[:, HDIM:].astype(jnp.bfloat16)
        q = q_ref[:, cut]
        g = g_ref[:, cut]
        scores = dot(split, jnp.concatenate([q, q], axis=1), 1, 1)
        scores = scores.reshape(total_rows // SLOTS, SLOTS, tokens)
        scores = scores * (factor * math.log2(math.e)) + bias[None]
        top = jnp.max(jnp.max(scores, axis=0), axis=0, keepdims=True)
        expo = jnp.exp2(scores - top[None])
        total = jnp.sum(jnp.sum(expo, axis=0), axis=0, keepdims=True)
        probs = expo * (1.0 / total)[None]
        dprobs = dot(values, g, 1, 1).reshape(probs.shape)
        inner = jnp.sum(jnp.sum(probs * dprobs, axis=0), axis=0, keepdims=True)
        dscores = (probs * (dprobs - inner[None])).reshape(total_rows, tokens)
        dscores = dscores.astype(jnp.bfloat16)
        probs_b = probs.reshape(total_rows, tokens).astype(jnp.bfloat16)
        att_ref[:, cut] = dot(probs_b, values, 0, 0).astype(jnp.bfloat16)
        dq = dot(dscores, split, 0, 0)
        dq_ref[:, cut] = ((dq[:, :HDIM] + dq[:, HDIM:]) * factor).astype(jnp.bfloat16)
        sources = jnp.concatenate(
            [jnp.concatenate([q, blank], axis=1), jnp.concatenate([blank, g], axis=1)], axis=0
        )
        pair = dot(jnp.concatenate([dscores, probs_b], axis=1), sources, 1, 0)
        grads[step * group + i, :, :HDIM] = (pair[:, :HDIM] * factor).astype(jnp.bfloat16)
        grads[step * group + i, :, HDIM:] = pair[:, HDIM:].astype(jnp.bfloat16)

    @pl.when(step == steps - 1)
    def _():
        heads = grads.shape[0]
        chunk = 256

        @pl.loop(0, total_rows // chunk)
        def _(r):
            here = pl.ds(pl.multiple_of(r * chunk, chunk), chunk)
            total = dot(grads[0, here, :], weights[0], 1, 1)
            for i in range(1, heads):
                total = total + dot(grads[i, here, :], weights[i], 1, 1)
            total = total.astype(jnp.bfloat16)
            for quarter in range(4):
                part_ref[quarter, here, :] = total[:, quarter * LANES : (quarter + 1) * LANES]


def attend(group, counts, slot_map, rows, queries, grads, key_weight, value_weight):
    tokens, width = queries.shape
    enc = key_weight.shape[0]
    total_rows = rows.shape[1]
    heads = width // HDIM
    wide = group * HDIM
    column = lambda i: (0, i)
    return pl.pallas_call(
        functools.partial(attend_kernel, group),
        grid=(heads // group,),
        out_shape=[
            jax.ShapeDtypeStruct((tokens, width), jnp.bfloat16),
            jax.ShapeDtypeStruct((tokens, width), jnp.bfloat16),
            jax.ShapeDtypeStruct((4, total_rows, LANES), jnp.bfloat16),
        ],
        in_specs=[
            pl.BlockSpec(memory_space=pltpu.SMEM),
            pl.BlockSpec(memory_space=pltpu.SMEM),
            pl.BlockSpec((4, total_rows, LANES), lambda i: (0, 0, 0)),
            pl.BlockSpec((tokens, wide), column),
            pl.BlockSpec((tokens, wide), column),
            pl.BlockSpec((enc, wide), column),
            pl.BlockSpec((enc, wide), column),
        ],
        out_specs=[
            pl.BlockSpec((tokens, wide), column),
            pl.BlockSpec((tokens, wide), column),
            pl.BlockSpec((4, total_rows, LANES), lambda i: (0, 0, 0)),
        ],
        scratch_shapes=[
            pltpu.VMEM((heads, total_rows, 2 * HDIM), jnp.bfloat16),
            pltpu.VMEM((heads, 4 * LANES, 2 * HDIM), jnp.bfloat16),
        ],
        compiler_params=pltpu.CompilerParams(vmem_limit_bytes=48 * 2**20),
        name="attend_heads",
    )(counts, slot_map, rows, queries, grads, key_weight, value_weight)


def reduce_kernel(n_seq, block, part_ref, out_ref, a_buf, y_out, y_buf, done, a_send, a_recv, y_send, y_recv, s_send, s_recv):
    me, head, y, core, across, beside = positions(n_seq)
    greet(n_seq, me, head, across, beside)

    def rows_of(owner):
        return pl.ds(pl.multiple_of(owner * block, block), block)

    order = list(range(n_seq - 1, -1, -1))
    firsts = {}
    for k in order:
        owner = (me + k) % n_seq
        for row in (0, 1):
            copy = pltpu.make_async_remote_copy(
                src_ref=part_ref.at[row * CORES + 1 - core, rows_of(owner), :],
                dst_ref=a_buf.at[k, row],
                send_sem=a_send.at[k, row],
                recv_sem=a_recv.at[k, row],
                device_id=(me, beside),
                device_id_type=MESH_ID,
            )
            copy.start()
            firsts[k, row] = copy
    seconds = {}
    for k in order:
        owner = (me + k) % n_seq
        for row in (0, 1):
            firsts[k, row].wait_recv()
        mixed = part_ref[across, rows_of(owner), :].astype(jnp.float32) + a_buf[k, 1 - y].astype(jnp.float32)
        y_out[k] = mixed.astype(jnp.bfloat16)
        copy = pltpu.make_async_remote_copy(
            src_ref=y_out.at[k],
            dst_ref=y_buf.at[k],
            send_sem=y_send.at[k],
            recv_sem=y_recv.at[k],
            device_id=(me, across),
            device_id_type=MESH_ID,
        )
        copy.start()
        seconds[k] = copy
    thirds = {}
    for k in order:
        owner = (me + k) % n_seq
        seconds[k].wait_recv()
        total = (
            part_ref[head, rows_of(owner), :].astype(jnp.float32)
            + a_buf[k, y].astype(jnp.float32)
            + y_buf[k].astype(jnp.float32)
        ).astype(jnp.bfloat16)
        if k == 0:
            out_ref[me] = total
        else:
            done[k] = total
            copy = pltpu.make_async_remote_copy(
                src_ref=done.at[k],
                dst_ref=out_ref.at[me],
                send_sem=s_send.at[k],
                recv_sem=s_recv.at[k],
                device_id=(owner, head),
                device_id_type=MESH_ID,
            )
            copy.start()
            thirds[k] = copy
    for copy in thirds.values():
        copy.wait_recv()
    for copies in (firsts, seconds, thirds):
        for copy in copies.values():
            copy.wait_send()


def reduce_back(n_seq, block, partial):
    dma = pltpu.SemaphoreType.DMA
    tile = (block, LANES)
    return pl.pallas_call(
        functools.partial(reduce_kernel, n_seq, block),
        out_shape=jax.ShapeDtypeStruct((n_seq,) + tile, jnp.bfloat16),
        in_specs=[pl.BlockSpec(memory_space=VMEM)],
        out_specs=pl.BlockSpec(memory_space=VMEM),
        scratch_shapes=[
            pltpu.VMEM((n_seq, 2) + tile, jnp.bfloat16),
            pltpu.VMEM((n_seq,) + tile, jnp.bfloat16),
            pltpu.VMEM((n_seq,) + tile, jnp.bfloat16),
            pltpu.VMEM((n_seq,) + tile, jnp.bfloat16),
            dma((n_seq, 2)),
            dma((n_seq, 2)),
            dma((n_seq,)),
            dma((n_seq,)),
            dma((n_seq,)),
            dma((n_seq,)),
        ],
        compiler_params=pltpu.CompilerParams(
            collective_id=1, has_side_effects=True, vmem_limit_bytes=16 * 2**20
        ),
        name="reduce_rows",
    )(partial)


def per_device_kernels(n_seq, queries, neighbours, key_weight, value_weight, counts, slot_map, d_attended):
    positions_local = neighbours.shape[1]
    enc_local = neighbours.shape[3]
    block = positions_local * SLOTS
    rows = gather(n_seq, block, neighbours.reshape(n_seq * block, enc_local))
    attended, d_queries, partial = attend(
        2, counts, slot_map, rows, queries, d_attended, key_weight, value_weight
    )
    back = reduce_back(n_seq, block, partial)
    d_neighbours = back[:, :, :enc_local].reshape(neighbours.shape)
    return (attended, d_queries, d_neighbours)


def solution(mesh):
    n_seq, n_head = mesh.shape["seq"], mesh.shape["head"]
    block = NB_LEN * SLOTS // n_seq
    per_device = per_device_plain
    if n_head == 4 and block % 32 == 0:
        per_device = functools.partial(per_device_kernels, n_seq)
    in_specs = (
        P("seq", "head"),
        P(None, "seq", None, "head"),
        P(None, "head"),
        P(None, "head"),
        P("seq"),
        P("seq", None),
        P("seq", "head"),
    )
    out_specs = (P("seq", "head"), P("seq", "head"), P(None, "seq", None, "head"))
    return jax.shard_map(
        per_device, mesh=mesh, in_specs=in_specs, out_specs=out_specs, check_vma=False
    )
```

```python
import functools
import math

import jax
import jax.numpy as jnp
from jax import lax
from jax.experimental import pallas as pl
from jax.experimental.pallas import tpu as pltpu
from jax.sharding import PartitionSpec as P

HDIM = 128
SPAN = 64
NB_LEN = 128
MAX_NB = 4
CH_DEV = 2
SLOTS = 8
LANES = 128
CORES = 2
MESH_ID = pl.DeviceIdType.MESH
VMEM = pltpu.VMEM


def present_table(count_row, slot_row):
    chosen = slot_row.reshape(CH_DEV, MAX_NB)
    ranks = jnp.arange(MAX_NB, dtype=jnp.int32)
    valid = ranks[None, :] < count_row[:, None]
    slot_ids = jnp.arange(SLOTS, dtype=jnp.int32)
    hits = valid[:, :, None] & (chosen[:, :, None] == slot_ids[None, None, :])
    return jnp.any(hits, axis=1)


def per_device_plain(queries, neighbours, key_weight, value_weight, counts, slot_map, d_attended):
    total_rows = NB_LEN * SLOTS
    enc_local = neighbours.shape[3]
    width_local = key_weight.shape[1]
    heads_local = width_local // HDIM
    token_count = queries.shape[0]
    highest = lax.Precision.HIGHEST
    arrived = lax.all_to_all(neighbours, "seq", split_axis=0, concat_axis=1, tiled=True)
    flat_rows = arrived.reshape(total_rows, enc_local)
    portion = lax.all_gather(flat_rows, "head", axis=1, tiled=True)
    key_sum = jnp.dot(portion, key_weight, preferred_element_type=jnp.float32)
    value_sum = jnp.dot(portion, value_weight, preferred_element_type=jnp.float32)
    keys = key_sum.reshape(total_rows, heads_local, HDIM)
    values = value_sum.astype(jnp.bfloat16).reshape(total_rows, heads_local, HDIM)
    present = present_table(counts, slot_map[0])
    allowed = jnp.tile(jnp.repeat(present, SPAN, axis=0), (1, NB_LEN))
    factor = 1.0 / HDIM**0.5
    query_heads = queries.reshape(token_count, heads_local, HDIM)
    grad_heads = d_attended.reshape(token_count, heads_local, HDIM)
    scores = (
        jnp.einsum(
            "thd,rhd->htr",
            query_heads.astype(jnp.float32),
            keys,
            precision=highest,
            preferred_element_type=jnp.float32,
        )
        * factor
    )
    scores = jnp.where(allowed[None, :, :], scores, -jnp.inf)
    top = jnp.max(scores, axis=-1, keepdims=True)
    expo = jnp.exp(scores - top)
    probs = expo / jnp.sum(expo, axis=-1, keepdims=True)
    probs_b = probs.astype(jnp.bfloat16)
    attended = jnp.einsum("htr,rhd->thd", probs_b, values, preferred_element_type=jnp.float32)
    attended = attended.astype(jnp.bfloat16).reshape(token_count, width_local)
    dprobs = jnp.einsum("thd,rhd->htr", grad_heads, values, preferred_element_type=jnp.float32)
    inner = jnp.sum(probs * dprobs, axis=-1, keepdims=True)
    dscores = (probs * (dprobs - inner)).astype(jnp.bfloat16)
    d_queries = (
        jnp.einsum(
            "htr,rhd->thd",
            dscores.astype(jnp.float32),
            keys,
            precision=highest,
            preferred_element_type=jnp.float32,
        )
        * factor
    )
    d_queries = d_queries.astype(jnp.bfloat16).reshape(token_count, width_local)
    d_keys = (
        jnp.einsum("htr,thd->rhd", dscores, query_heads, preferred_element_type=jnp.float32)
        * factor
    )
    d_keys = d_keys.astype(jnp.bfloat16).reshape(total_rows, width_local)
    d_values = jnp.einsum("htr,thd->rhd", probs_b, grad_heads, preferred_element_type=jnp.float32)
    d_values = d_values.astype(jnp.bfloat16).reshape(total_rows, width_local)
    contract = (((1,), (1,)), ((), ()))
    partial_value = lax.dot_general(
        d_keys, key_weight, contract, preferred_element_type=jnp.float32
    )
    partial_value = partial_value + lax.dot_general(
        d_values, value_weight, contract, preferred_element_type=jnp.float32
    )
    summed = lax.psum(partial_value.astype(jnp.bfloat16), "head").astype(jnp.float32)
    own_part = lax.dynamic_slice_in_dim(summed, lax.axis_index("head") * enc_local, enc_local, 1)
    grad_rows = own_part.astype(jnp.bfloat16).reshape(1, NB_LEN, SLOTS, enc_local)
    d_neighbours = lax.all_to_all(grad_rows, "seq", split_axis=1, concat_axis=0, tiled=True)
    return (attended, d_queries, d_neighbours)


def positions(n_seq):
    me = lax.axis_index("seq")
    head = lax.axis_index("head")
    y = head // CORES
    core = head % CORES
    across = (1 - y) * CORES + core
    beside = y * CORES + (1 - core)
    return me, head, y, core, across, beside


def greet(n_seq, me, head, across, beside):
    barrier = pltpu.get_barrier_semaphore()
    for k in range(1, n_seq):
        pl.semaphore_signal(
            barrier, inc=1, device_id=((me + k) % n_seq, head), device_id_type=MESH_ID
        )
    for peer in (across, beside):
        pl.semaphore_signal(barrier, inc=1, device_id=(me, peer), device_id_type=MESH_ID)
    pl.semaphore_wait(barrier, n_seq + 1)


def gather_kernel(n_seq, block, nb_ref, rows_ref, own_sem, s_send, s_recv, y_send, y_recv, c_send, c_recv, f_send, f_recv):
    me, head, y, core, across, beside = positions(n_seq)
    greet(n_seq, me, head, across, beside)

    def rows_of(quarter, owner):
        return rows_ref.at[quarter, :, pl.ds(pl.multiple_of(owner * block, block), block), :]

    def remote(src, dst, send, recv, device):
        return pltpu.make_async_remote_copy(
            src_ref=src,
            dst_ref=dst,
            send_sem=send,
            recv_sem=recv,
            device_id=device,
            device_id_type=MESH_ID,
        )

    own = pltpu.make_async_copy(
        nb_ref.at[me], rows_of(head, me), own_sem
    )
    own.start()
    sent = []
    for k in range(n_seq - 1, 0, -1):
        to = (me + k) % n_seq
        copy = remote(
            nb_ref.at[to],
            rows_of(head, me),
            s_send.at[k],
            s_recv.at[k],
            (to, head),
        )
        copy.start()
        sent.append((k, copy))
    pending = []
    order = [0] + [k for k, _ in sent]
    arrivals = dict(sent)
    own.wait()
    for k in order:
        owner = (me + n_seq - k) % n_seq
        if k > 0:
            arrivals[k].wait_recv()
        over = remote(rows_of(head, owner), rows_of(head, owner), y_send.at[k], y_recv.at[k], (me, across))
        over.start()
        side = remote(rows_of(head, owner), rows_of(head, owner), c_send.at[k], c_recv.at[k], (me, beside))
        side.start()
        pending.append((owner, k, over, side))
    forwards = []
    for owner, k, over, side in pending:
        over.wait_recv()
        forward = remote(
            rows_of(across, owner), rows_of(across, owner), f_send.at[k], f_recv.at[k], (me, beside)
        )
        forward.start()
        forwards.append(forward)
    for owner, k, over, side in pending:
        side.wait_recv()
    for forward in forwards:
        forward.wait_recv()
    for k, copy in sent:
        copy.wait_send()
    for owner, k, over, side in pending:
        over.wait_send()
        side.wait_send()
    for forward in forwards:
        forward.wait_send()


def gather(n_seq, block, rows):
    dma = pltpu.SemaphoreType.DMA
    return pl.pallas_call(
        functools.partial(gather_kernel, n_seq, block),
        out_shape=jax.ShapeDtypeStruct((4, SLOTS, n_seq * block, LANES), jnp.bfloat16),
        in_specs=[pl.BlockSpec(memory_space=VMEM)],
        out_specs=pl.BlockSpec(memory_space=VMEM),
        scratch_shapes=[dma] + [dma((n_seq,)) for _ in range(8)],
        compiler_params=pltpu.CompilerParams(
            collective_id=0, has_side_effects=True, vmem_limit_bytes=16 * 2**20
        ),
        cost_estimate=pl.CostEstimate(flops=0, bytes_accessed=40 * 2**20, transcendentals=0),
        name="gather_rows",
    )(rows)


def dot(a, b, left, right):
    return lax.dot_general(
        a, b, (((left,), (right,)), ((), ())), preferred_element_type=jnp.float32
    )


def padded(weight, enc_local):
    gap = jnp.zeros((LANES - enc_local, weight.shape[1]), weight.dtype)
    parts = []
    for quarter in range(4):
        parts += [weight[quarter * enc_local : (quarter + 1) * enc_local], gap]
    return jnp.concatenate(parts, axis=0)


def attend_kernel(group, counts_ref, slots_ref, rows_ref, q_ref, g_ref, wk_ref, wv_ref, att_ref, dq_ref, part_ref, grads, weights):
    step = pl.program_id(0)
    steps = pl.num_programs(0)
    length = rows_ref.shape[2]
    half = MAX_NB * length
    enc_local = wk_ref.shape[0] // 4
    tokens = q_ref.shape[0]
    factor = 1.0 / HDIM**0.5
    late = lax.broadcasted_iota(jnp.int32, (1, tokens), 1) >= SPAN
    own_count = jnp.where(late, counts_ref[1], counts_ref[0])
    bias = [jnp.where(j < own_count, 0.0, -jnp.inf)[None] for j in range(MAX_NB)]
    bias = jnp.concatenate(bias, axis=0)
    slots = [slots_ref[0, i] for i in range(SLOTS)]
    rows = jnp.concatenate(
        [
            jnp.concatenate([rows_ref[quarter, slots[i]] for quarter in range(4)], axis=1)
            for i in range(SLOTS)
        ],
        axis=0,
    )
    blank = jnp.zeros((SPAN, HDIM), jnp.bfloat16)

    def spread(x):
        return jnp.concatenate(
            [
                jnp.concatenate([x[:SPAN], blank], axis=1),
                jnp.concatenate([blank, x[SPAN:]], axis=1),
            ],
            axis=0,
        )

    def beside_each_other(x):
        return jnp.concatenate([x[:half], x[half:]], axis=1)

    def diagonal(x):
        return jnp.concatenate([x[:SPAN, :HDIM], x[SPAN:, HDIM:]], axis=0)

    for i in range(group):
        cut = slice(i * HDIM, (i + 1) * HDIM)
        weight = padded(
            jnp.concatenate([wk_ref[:, cut], wv_ref[:, cut]], axis=1), enc_local
        )
        weights[step * group + i] = weight
        both = dot(rows, weight, 1, 0)
        keys = beside_each_other(both[:, :HDIM])
        keys_high = keys.astype(jnp.bfloat16)
        keys_low = (keys - keys_high.astype(jnp.float32)).astype(jnp.bfloat16)
        values = beside_each_other(both[:, HDIM:]).astype(jnp.bfloat16)
        q = spread(q_ref[:, cut])
        g = spread(g_ref[:, cut])
        scores = dot(keys_high, q, 1, 1) + dot(keys_low, q, 1, 1)
        scores = scores.reshape(MAX_NB, length, tokens)
        scores = scores * (factor * math.log2(math.e)) + bias
        top = jnp.max(jnp.max(scores, axis=0), axis=0, keepdims=True)
        expo = jnp.exp2(scores - top[None])
        total = jnp.sum(jnp.sum(expo, axis=0), axis=0, keepdims=True)
        probs = expo * (1.0 / total)[None]
        dprobs = dot(values, g, 1, 1).reshape(probs.shape)
        inner = jnp.sum(jnp.sum(probs * dprobs, axis=0), axis=0, keepdims=True)
        dscores = (probs * (dprobs - inner[None])).reshape(half, tokens)
        dscores = dscores.astype(jnp.bfloat16)
        probs_b = probs.reshape(half, tokens).astype(jnp.bfloat16)
        att_ref[:, cut] = diagonal(dot(probs_b, values, 0, 0)).astype(jnp.bfloat16)
        dq = diagonal(dot(dscores, keys_high, 0, 0) + dot(dscores, keys_low, 0, 0))
        dq_ref[:, cut] = (dq * factor).astype(jnp.bfloat16)
        d_keys = (dot(dscores, q, 1, 0) * factor).astype(jnp.bfloat16)
        d_values = dot(probs_b, g, 1, 0).astype(jnp.bfloat16)
        for c in range(CH_DEV):
            part = slice(c * half, (c + 1) * half)
            side = slice(c * HDIM, (c + 1) * HDIM)
            grads[step * group + i, part, :HDIM] = d_keys[:, side]
            grads[step * group + i, part, HDIM:] = d_values[:, side]

    @pl.when(step == steps - 1)
    def _():
        heads = grads.shape[0]
        chunk = 2 * length

        @pl.loop(0, SLOTS // 2)
        def _(r):
            here = pl.ds(pl.multiple_of(r * chunk, chunk), chunk)
            total = dot(grads[0, here, :], weights[0], 1, 1)
            for i in range(1, heads):
                total = total + dot(grads[i, here, :], weights[i], 1, 1)
            total = total.astype(jnp.bfloat16)
            for row in range(2):
                slot = slots_ref[0, 2 * r + row]
                for quarter in range(4):
                    part_ref[quarter, slot] = total[
                        row * length : (row + 1) * length, quarter * LANES : (quarter + 1) * LANES
                    ]


def attend(group, counts, slot_map, rows, queries, grads, key_weight, value_weight):
    tokens, width = queries.shape
    enc = key_weight.shape[0]
    length = rows.shape[2]
    heads = width // HDIM
    whole = (4, SLOTS, length, LANES)
    wide = group * HDIM
    column = lambda i: (0, i)
    return pl.pallas_call(
        functools.partial(attend_kernel, group),
        grid=(heads // group,),
        out_shape=[
            jax.ShapeDtypeStruct((tokens, width), jnp.bfloat16),
            jax.ShapeDtypeStruct((tokens, width), jnp.bfloat16),
            jax.ShapeDtypeStruct(whole, jnp.bfloat16),
        ],
        in_specs=[
            pl.BlockSpec(memory_space=pltpu.SMEM),
            pl.BlockSpec(memory_space=pltpu.SMEM),
            pl.BlockSpec(whole, lambda i: (0, 0, 0, 0)),
            pl.BlockSpec((tokens, wide), column),
            pl.BlockSpec((tokens, wide), column),
            pl.BlockSpec((enc, wide), column),
            pl.BlockSpec((enc, wide), column),
        ],
        out_specs=[
            pl.BlockSpec((tokens, wide), column),
            pl.BlockSpec((tokens, wide), column),
            pl.BlockSpec(whole, lambda i: (0, 0, 0, 0)),
        ],
        scratch_shapes=[
            pltpu.VMEM((heads, SLOTS * length, 2 * HDIM), jnp.bfloat16),
            pltpu.VMEM((heads, 4 * LANES, 2 * HDIM), jnp.bfloat16),
        ],
        compiler_params=pltpu.CompilerParams(vmem_limit_bytes=48 * 2**20),
        name="attend_heads",
    )(counts, slot_map, rows, queries, grads, key_weight, value_weight)


def reduce_kernel(n_seq, block, part_ref, out_ref, a_buf, y_out, y_buf, done, a_send, a_recv, y_send, y_recv, s_send, s_recv):
    me, head, y, core, across, beside = positions(n_seq)
    greet(n_seq, me, head, across, beside)

    def rows_of(owner):
        return pl.ds(pl.multiple_of(owner * block, block), block)

    order = list(range(n_seq - 1, -1, -1))
    firsts = {}
    for k in order:
        owner = (me + k) % n_seq
        for row in (0, 1):
            copy = pltpu.make_async_remote_copy(
                src_ref=part_ref.at[row * CORES + 1 - core, :, rows_of(owner), :],
                dst_ref=a_buf.at[k, row],
                send_sem=a_send.at[k, row],
                recv_sem=a_recv.at[k, row],
                device_id=(me, beside),
                device_id_type=MESH_ID,
            )
            copy.start()
            firsts[k, row] = copy
    seconds = {}
    for k in order:
        owner = (me + k) % n_seq
        for row in (0, 1):
            firsts[k, row].wait_recv()
        mixed = part_ref[across, :, rows_of(owner), :].astype(jnp.float32) + a_buf[k, 1 - y].astype(jnp.float32)
        y_out[k] = mixed.astype(jnp.bfloat16)
        copy = pltpu.make_async_remote_copy(
            src_ref=y_out.at[k],
            dst_ref=y_buf.at[k],
            send_sem=y_send.at[k],
            recv_sem=y_recv.at[k],
            device_id=(me, across),
            device_id_type=MESH_ID,
        )
        copy.start()
        seconds[k] = copy
    thirds = {}
    for k in order:
        owner = (me + k) % n_seq
        seconds[k].wait_recv()
        total = (
            part_ref[head, :, rows_of(owner), :].astype(jnp.float32)
            + a_buf[k, y].astype(jnp.float32)
            + y_buf[k].astype(jnp.float32)
        ).astype(jnp.bfloat16)
        if k == 0:
            out_ref[me] = total
        else:
            done[k] = total
            copy = pltpu.make_async_remote_copy(
                src_ref=done.at[k],
                dst_ref=out_ref.at[me],
                send_sem=s_send.at[k],
                recv_sem=s_recv.at[k],
                device_id=(owner, head),
                device_id_type=MESH_ID,
            )
            copy.start()
            thirds[k] = copy
    for copy in thirds.values():
        copy.wait_recv()
    for copies in (firsts, seconds, thirds):
        for copy in copies.values():
            copy.wait_send()


def reduce_back(n_seq, block, partial):
    dma = pltpu.SemaphoreType.DMA
    tile = (SLOTS, block, LANES)
    return pl.pallas_call(
        functools.partial(reduce_kernel, n_seq, block),
        out_shape=jax.ShapeDtypeStruct((n_seq,) + tile, jnp.bfloat16),
        in_specs=[pl.BlockSpec(memory_space=VMEM)],
        out_specs=pl.BlockSpec(memory_space=VMEM),
        scratch_shapes=[
            pltpu.VMEM((n_seq, 2) + tile, jnp.bfloat16),
            pltpu.VMEM((n_seq,) + tile, jnp.bfloat16),
            pltpu.VMEM((n_seq,) + tile, jnp.bfloat16),
            pltpu.VMEM((n_seq,) + tile, jnp.bfloat16),
            dma((n_seq, 2)),
            dma((n_seq, 2)),
            dma((n_seq,)),
            dma((n_seq,)),
            dma((n_seq,)),
            dma((n_seq,)),
        ],
        compiler_params=pltpu.CompilerParams(
            collective_id=1, has_side_effects=True, vmem_limit_bytes=16 * 2**20
        ),
        name="reduce_rows",
    )(partial)


def per_device_kernels(n_seq, queries, neighbours, key_weight, value_weight, counts, slot_map, d_attended):
    block = neighbours.shape[1]
    enc_local = neighbours.shape[3]
    by_slot = jnp.pad(
        neighbours.transpose(0, 2, 1, 3), ((0, 0), (0, 0), (0, 0), (0, LANES - enc_local))
    )
    rows = gather(n_seq, block, by_slot)
    attended, d_queries, partial = attend(
        2, counts, slot_map, rows, queries, d_attended, key_weight, value_weight
    )
    back = reduce_back(n_seq, block, partial)
    d_neighbours = back[:, :, :, :enc_local].transpose(0, 2, 1, 3)
    return (attended, d_queries, d_neighbours)


def solution(mesh):
    n_seq, n_head = mesh.shape["seq"], mesh.shape["head"]
    block = NB_LEN // n_seq
    per_device = per_device_plain
    if n_head == 4 and block % 16 == 0:
        per_device = functools.partial(per_device_kernels, n_seq)
    in_specs = (
        P("seq", "head"),
        P(None, "seq", None, "head"),
        P(None, "head"),
        P(None, "head"),
        P("seq"),
        P("seq", None),
        P("seq", "head"),
    )
    out_specs = (P("seq", "head"), P("seq", "head"), P(None, "seq", None, "head"))
    return jax.shard_map(
        per_device, mesh=mesh, in_specs=in_specs, out_specs=out_specs, check_vma=False
    )
```

```python
import functools
import math

import jax
import jax.numpy as jnp
from jax import lax
from jax.experimental import pallas as pl
from jax.experimental.pallas import tpu as pltpu
from jax.sharding import PartitionSpec as P

HDIM = 128
SPAN = 64
NB_LEN = 128
MAX_NB = 4
CH_DEV = 2
SLOTS = 8
LANES = 128
CORES = 2
MESH_ID = pl.DeviceIdType.MESH
VMEM = pltpu.VMEM


def present_table(count_row, slot_row):
    chosen = slot_row.reshape(CH_DEV, MAX_NB)
    ranks = jnp.arange(MAX_NB, dtype=jnp.int32)
    valid = ranks[None, :] < count_row[:, None]
    slot_ids = jnp.arange(SLOTS, dtype=jnp.int32)
    hits = valid[:, :, None] & (chosen[:, :, None] == slot_ids[None, None, :])
    return jnp.any(hits, axis=1)


def per_device_plain(queries, neighbours, key_weight, value_weight, counts, slot_map, d_attended):
    total_rows = NB_LEN * SLOTS
    enc_local = neighbours.shape[3]
    width_local = key_weight.shape[1]
    heads_local = width_local // HDIM
    token_count = queries.shape[0]
    highest = lax.Precision.HIGHEST
    arrived = lax.all_to_all(neighbours, "seq", split_axis=0, concat_axis=1, tiled=True)
    flat_rows = arrived.reshape(total_rows, enc_local)
    portion = lax.all_gather(flat_rows, "head", axis=1, tiled=True)
    key_sum = jnp.dot(portion, key_weight, preferred_element_type=jnp.float32)
    value_sum = jnp.dot(portion, value_weight, preferred_element_type=jnp.float32)
    keys = key_sum.reshape(total_rows, heads_local, HDIM)
    values = value_sum.astype(jnp.bfloat16).reshape(total_rows, heads_local, HDIM)
    present = present_table(counts, slot_map[0])
    allowed = jnp.tile(jnp.repeat(present, SPAN, axis=0), (1, NB_LEN))
    factor = 1.0 / HDIM**0.5
    query_heads = queries.reshape(token_count, heads_local, HDIM)
    grad_heads = d_attended.reshape(token_count, heads_local, HDIM)
    scores = (
        jnp.einsum(
            "thd,rhd->htr",
            query_heads.astype(jnp.float32),
            keys,
            precision=highest,
            preferred_element_type=jnp.float32,
        )
        * factor
    )
    scores = jnp.where(allowed[None, :, :], scores, -jnp.inf)
    top = jnp.max(scores, axis=-1, keepdims=True)
    expo = jnp.exp(scores - top)
    probs = expo / jnp.sum(expo, axis=-1, keepdims=True)
    probs_b = probs.astype(jnp.bfloat16)
    attended = jnp.einsum("htr,rhd->thd", probs_b, values, preferred_element_type=jnp.float32)
    attended = attended.astype(jnp.bfloat16).reshape(token_count, width_local)
    dprobs = jnp.einsum("thd,rhd->htr", grad_heads, values, preferred_element_type=jnp.float32)
    inner = jnp.sum(probs * dprobs, axis=-1, keepdims=True)
    dscores = (probs * (dprobs - inner)).astype(jnp.bfloat16)
    d_queries = (
        jnp.einsum(
            "htr,rhd->thd",
            dscores.astype(jnp.float32),
            keys,
            precision=highest,
            preferred_element_type=jnp.float32,
        )
        * factor
    )
    d_queries = d_queries.astype(jnp.bfloat16).reshape(token_count, width_local)
    d_keys = (
        jnp.einsum("htr,thd->rhd", dscores, query_heads, preferred_element_type=jnp.float32)
        * factor
    )
    d_keys = d_keys.astype(jnp.bfloat16).reshape(total_rows, width_local)
    d_values = jnp.einsum("htr,thd->rhd", probs_b, grad_heads, preferred_element_type=jnp.float32)
    d_values = d_values.astype(jnp.bfloat16).reshape(total_rows, width_local)
    contract = (((1,), (1,)), ((), ()))
    partial_value = lax.dot_general(
        d_keys, key_weight, contract, preferred_element_type=jnp.float32
    )
    partial_value = partial_value + lax.dot_general(
        d_values, value_weight, contract, preferred_element_type=jnp.float32
    )
    summed = lax.psum(partial_value.astype(jnp.bfloat16), "head").astype(jnp.float32)
    own_part = lax.dynamic_slice_in_dim(summed, lax.axis_index("head") * enc_local, enc_local, 1)
    grad_rows = own_part.astype(jnp.bfloat16).reshape(1, NB_LEN, SLOTS, enc_local)
    d_neighbours = lax.all_to_all(grad_rows, "seq", split_axis=1, concat_axis=0, tiled=True)
    return (attended, d_queries, d_neighbours)


def positions(n_seq):
    me = lax.axis_index("seq")
    head = lax.axis_index("head")
    y = head // CORES
    core = head % CORES
    across = (1 - y) * CORES + core
    beside = y * CORES + (1 - core)
    return me, head, y, core, across, beside


def greet(n_seq, me, head, across, beside):
    barrier = pltpu.get_barrier_semaphore()
    for k in range(1, n_seq):
        pl.semaphore_signal(
            barrier, inc=1, device_id=((me + k) % n_seq, head), device_id_type=MESH_ID
        )
    for peer in (across, beside):
        pl.semaphore_signal(barrier, inc=1, device_id=(me, peer), device_id_type=MESH_ID)
    pl.semaphore_wait(barrier, n_seq + 1)


def gather_kernel(n_seq, block, nb_ref, rows_ref, own_sem, s_send, s_recv, y_send, y_recv, c_send, c_recv, f_send, f_recv):
    me, head, y, core, across, beside = positions(n_seq)
    greet(n_seq, me, head, across, beside)

    def rows_of(quarter, owner):
        return rows_ref.at[quarter, :, pl.ds(pl.multiple_of(owner * block, block), block), :]

    def remote(src, dst, send, recv, device):
        return pltpu.make_async_remote_copy(
            src_ref=src,
            dst_ref=dst,
            send_sem=send,
            recv_sem=recv,
            device_id=device,
            device_id_type=MESH_ID,
        )

    own = pltpu.make_async_copy(
        nb_ref.at[me], rows_of(head, me), own_sem
    )
    own.start()
    sent = []
    for k in range(n_seq - 1, 0, -1):
        to = (me + k) % n_seq
        copy = remote(
            nb_ref.at[to],
            rows_of(head, me),
            s_send.at[k],
            s_recv.at[k],
            (to, head),
        )
        copy.start()
        sent.append((k, copy))
    pending = []
    order = [0] + [k for k, _ in sent]
    arrivals = dict(sent)
    own.wait()
    for k in order:
        owner = (me + n_seq - k) % n_seq
        if k > 0:
            arrivals[k].wait_recv()
        over = remote(rows_of(head, owner), rows_of(head, owner), y_send.at[k], y_recv.at[k], (me, across))
        over.start()
        side = remote(rows_of(head, owner), rows_of(head, owner), c_send.at[k], c_recv.at[k], (me, beside))
        side.start()
        pending.append((owner, k, over, side))
    forwards = []
    for owner, k, over, side in pending:
        over.wait_recv()
        forward = remote(
            rows_of(across, owner), rows_of(across, owner), f_send.at[k], f_recv.at[k], (me, beside)
        )
        forward.start()
        forwards.append(forward)
    for owner, k, over, side in pending:
        side.wait_recv()
    for forward in forwards:
        forward.wait_recv()
    for k, copy in sent:
        copy.wait_send()
    for owner, k, over, side in pending:
        over.wait_send()
        side.wait_send()
    for forward in forwards:
        forward.wait_send()


def gather(n_seq, block, rows):
    dma = pltpu.SemaphoreType.DMA
    return pl.pallas_call(
        functools.partial(gather_kernel, n_seq, block),
        out_shape=jax.ShapeDtypeStruct((4, SLOTS, n_seq * block, LANES), jnp.bfloat16),
        in_specs=[pl.BlockSpec(memory_space=VMEM)],
        out_specs=pl.BlockSpec(memory_space=VMEM),
        scratch_shapes=[dma] + [dma((n_seq,)) for _ in range(8)],
        compiler_params=pltpu.CompilerParams(
            collective_id=0, has_side_effects=True, vmem_limit_bytes=16 * 2**20
        ),
        cost_estimate=pl.CostEstimate(flops=0, bytes_accessed=40 * 2**20, transcendentals=0),
        name="gather_rows",
    )(rows)


def dot(a, b, left, right):
    return lax.dot_general(
        a, b, (((left,), (right,)), ((), ())), preferred_element_type=jnp.float32
    )


def padded(weight, enc_local):
    gap = jnp.zeros((LANES - enc_local, weight.shape[1]), weight.dtype)
    parts = []
    for quarter in range(4):
        parts += [weight[quarter * enc_local : (quarter + 1) * enc_local], gap]
    return jnp.concatenate(parts, axis=0)


def attend_kernel(group, counts_ref, slots_ref, rows_ref, q_ref, g_ref, wk_ref, wv_ref, att_ref, dq_ref, part_ref, grads, weights, rows):
    step = pl.program_id(0)
    steps = pl.num_programs(0)
    length = rows_ref.shape[2]
    half = MAX_NB * length
    enc_local = wk_ref.shape[0] // 4
    tokens = q_ref.shape[0]
    factor = 1.0 / HDIM**0.5
    late = lax.broadcasted_iota(jnp.int32, (1, tokens), 1) >= SPAN
    own_count = jnp.where(late, counts_ref[1], counts_ref[0])
    bias = [jnp.where(j < own_count, 0.0, -jnp.inf)[None] for j in range(MAX_NB)]
    bias = jnp.concatenate(bias, axis=0)
    slots = [slots_ref[0, i] for i in range(SLOTS)]

    @pl.when(step == 0)
    def _():
        for i in range(SLOTS):
            for quarter in range(4):
                rows[
                    i * length : (i + 1) * length, quarter * LANES : (quarter + 1) * LANES
                ] = rows_ref[quarter, slots[i]]

    blank = jnp.zeros((SPAN, HDIM), jnp.bfloat16)

    def spread(x):
        return jnp.concatenate(
            [
                jnp.concatenate([x[:SPAN], blank], axis=1),
                jnp.concatenate([blank, x[SPAN:]], axis=1),
            ],
            axis=0,
        )

    def beside_each_other(x):
        return jnp.concatenate([x[:half], x[half:]], axis=1)

    def diagonal(x):
        return jnp.concatenate([x[:SPAN, :HDIM], x[SPAN:, HDIM:]], axis=0)

    for i in range(group):
        cut = slice(i * HDIM, (i + 1) * HDIM)
        weight = padded(
            jnp.concatenate([wk_ref[:, cut], wv_ref[:, cut]], axis=1), enc_local
        )
        head = step * group + i
        lanes = pl.ds(pl.multiple_of(head * 2 * HDIM, 2 * HDIM), 2 * HDIM)
        weights[:, lanes] = weight
        both = dot(rows[...], weight, 1, 0)
        keys = beside_each_other(both[:, :HDIM])
        keys_high = keys.astype(jnp.bfloat16)
        keys_low = (keys - keys_high.astype(jnp.float32)).astype(jnp.bfloat16)
        values = beside_each_other(both[:, HDIM:]).astype(jnp.bfloat16)
        q = spread(q_ref[:, cut])
        g = spread(g_ref[:, cut])
        split = jnp.concatenate([keys_high, keys_low], axis=1)
        scores = dot(split, jnp.concatenate([q, q], axis=1), 1, 1)
        scores = scores.reshape(MAX_NB, length, tokens)
        scores = scores * (factor * math.log2(math.e)) + bias
        top = jnp.max(jnp.max(scores, axis=0), axis=0, keepdims=True)
        expo = jnp.exp2(scores - top[None])
        total = jnp.sum(jnp.sum(expo, axis=0), axis=0, keepdims=True)
        probs = expo * (1.0 / total)[None]
        dprobs = dot(values, g, 1, 1).reshape(probs.shape)
        inner = jnp.sum(jnp.sum(probs * dprobs, axis=0), axis=0, keepdims=True)
        dscores = (probs * (dprobs - inner[None])).reshape(half, tokens)
        dscores = dscores.astype(jnp.bfloat16)
        probs_b = probs.reshape(half, tokens).astype(jnp.bfloat16)
        att_ref[:, cut] = diagonal(dot(probs_b, values, 0, 0)).astype(jnp.bfloat16)
        dq = diagonal(dot(dscores, keys_high, 0, 0) + dot(dscores, keys_low, 0, 0))
        dq_ref[:, cut] = (dq * factor).astype(jnp.bfloat16)
        d_keys = (dot(dscores, q, 1, 0) * factor).astype(jnp.bfloat16)
        d_values = dot(probs_b, g, 1, 0).astype(jnp.bfloat16)
        pair = [
            jnp.concatenate(
                [d_keys[:, c * HDIM : (c + 1) * HDIM], d_values[:, c * HDIM : (c + 1) * HDIM]], axis=1
            )
            for c in range(CH_DEV)
        ]
        grads[:, lanes] = jnp.concatenate(pair, axis=0)

    @pl.when(step == steps - 1)
    def _():
        chunk = 2 * length

        @pl.loop(0, SLOTS // 2)
        def _(r):
            here = pl.ds(pl.multiple_of(r * chunk, chunk), chunk)
            total = dot(grads[here, :], weights[...], 1, 1)
            total = total.astype(jnp.bfloat16)
            for row in range(2):
                slot = slots_ref[0, 2 * r + row]
                for quarter in range(4):
                    part_ref[quarter, slot] = total[
                        row * length : (row + 1) * length, quarter * LANES : (quarter + 1) * LANES
                    ]


def attend(group, counts, slot_map, rows, queries, grads, key_weight, value_weight):
    tokens, width = queries.shape
    enc = key_weight.shape[0]
    length = rows.shape[2]
    heads = width // HDIM
    whole = (4, SLOTS, length, LANES)
    wide = group * HDIM
    column = lambda i: (0, i)
    return pl.pallas_call(
        functools.partial(attend_kernel, group),
        grid=(heads // group,),
        out_shape=[
            jax.ShapeDtypeStruct((tokens, width), jnp.bfloat16),
            jax.ShapeDtypeStruct((tokens, width), jnp.bfloat16),
            jax.ShapeDtypeStruct(whole, jnp.bfloat16),
        ],
        in_specs=[
            pl.BlockSpec(memory_space=pltpu.SMEM),
            pl.BlockSpec(memory_space=pltpu.SMEM),
            pl.BlockSpec(whole, lambda i: (0, 0, 0, 0)),
            pl.BlockSpec((tokens, wide), column),
            pl.BlockSpec((tokens, wide), column),
            pl.BlockSpec((enc, wide), column),
            pl.BlockSpec((enc, wide), column),
        ],
        out_specs=[
            pl.BlockSpec((tokens, wide), column),
            pl.BlockSpec((tokens, wide), column),
            pl.BlockSpec(whole, lambda i: (0, 0, 0, 0)),
        ],
        scratch_shapes=[
            pltpu.VMEM((SLOTS * length, 2 * width), jnp.bfloat16),
            pltpu.VMEM((4 * LANES, 2 * width), jnp.bfloat16),
            pltpu.VMEM((SLOTS * length, 4 * LANES), jnp.bfloat16),
        ],
        compiler_params=pltpu.CompilerParams(vmem_limit_bytes=48 * 2**20),
        name="attend_heads",
    )(counts, slot_map, rows, queries, grads, key_weight, value_weight)


def reduce_kernel(n_seq, block, part_ref, out_ref, a_buf, y_out, y_buf, done, a_send, a_recv, y_send, y_recv, s_send, s_recv):
    me, head, y, core, across, beside = positions(n_seq)
    greet(n_seq, me, head, across, beside)

    def rows_of(owner):
        return pl.ds(pl.multiple_of(owner * block, block), block)

    order = sorted(range(n_seq), key=lambda k: -min(k, n_seq - k))
    firsts = {}
    for k in order:
        owner = (me + k) % n_seq
        for row in (0, 1):
            copy = pltpu.make_async_remote_copy(
                src_ref=part_ref.at[row * CORES + 1 - core, :, rows_of(owner), :],
                dst_ref=a_buf.at[k, row],
                send_sem=a_send.at[k, row],
                recv_sem=a_recv.at[k, row],
                device_id=(me, beside),
                device_id_type=MESH_ID,
            )
            copy.start()
            firsts[k, row] = copy
    seconds = {}
    for k in order:
        owner = (me + k) % n_seq
        for row in (0, 1):
            firsts[k, row].wait_recv()
        mixed = part_ref[across, :, rows_of(owner), :].astype(jnp.float32) + a_buf[k, 1 - y].astype(jnp.float32)
        y_out[k] = mixed.astype(jnp.bfloat16)
        copy = pltpu.make_async_remote_copy(
            src_ref=y_out.at[k],
            dst_ref=y_buf.at[k],
            send_sem=y_send.at[k],
            recv_sem=y_recv.at[k],
            device_id=(me, across),
            device_id_type=MESH_ID,
        )
        copy.start()
        seconds[k] = copy
    thirds = {}
    for k in order:
        owner = (me + k) % n_seq
        seconds[k].wait_recv()
        total = (
            part_ref[head, :, rows_of(owner), :].astype(jnp.float32)
            + a_buf[k, y].astype(jnp.float32)
            + y_buf[k].astype(jnp.float32)
        ).astype(jnp.bfloat16)
        if k == 0:
            out_ref[me] = total
        else:
            done[k] = total
            copy = pltpu.make_async_remote_copy(
                src_ref=done.at[k],
                dst_ref=out_ref.at[me],
                send_sem=s_send.at[k],
                recv_sem=s_recv.at[k],
                device_id=(owner, head),
                device_id_type=MESH_ID,
            )
            copy.start()
            thirds[k] = copy
    for copy in thirds.values():
        copy.wait_recv()
    for copies in (firsts, seconds, thirds):
        for copy in copies.values():
            copy.wait_send()


def reduce_back(n_seq, block, partial):
    dma = pltpu.SemaphoreType.DMA
    tile = (SLOTS, block, LANES)
    return pl.pallas_call(
        functools.partial(reduce_kernel, n_seq, block),
        out_shape=jax.ShapeDtypeStruct((n_seq,) + tile, jnp.bfloat16),
        in_specs=[pl.BlockSpec(memory_space=VMEM)],
        out_specs=pl.BlockSpec(memory_space=VMEM),
        scratch_shapes=[
            pltpu.VMEM((n_seq, 2) + tile, jnp.bfloat16),
            pltpu.VMEM((n_seq,) + tile, jnp.bfloat16),
            pltpu.VMEM((n_seq,) + tile, jnp.bfloat16),
            pltpu.VMEM((n_seq,) + tile, jnp.bfloat16),
            dma((n_seq, 2)),
            dma((n_seq, 2)),
            dma((n_seq,)),
            dma((n_seq,)),
            dma((n_seq,)),
            dma((n_seq,)),
        ],
        compiler_params=pltpu.CompilerParams(
            collective_id=1, has_side_effects=True, vmem_limit_bytes=16 * 2**20
        ),
        name="reduce_rows",
    )(partial)


def per_device_kernels(n_seq, queries, neighbours, key_weight, value_weight, counts, slot_map, d_attended):
    block = neighbours.shape[1]
    enc_local = neighbours.shape[3]
    by_slot = jnp.pad(
        neighbours.transpose(0, 2, 1, 3), ((0, 0), (0, 0), (0, 0), (0, LANES - enc_local))
    )
    rows = gather(n_seq, block, by_slot)
    attended, d_queries, partial = attend(
        2, counts, slot_map, rows, queries, d_attended, key_weight, value_weight
    )
    back = reduce_back(n_seq, block, partial)
    d_neighbours = back[:, :, :, :enc_local].transpose(0, 2, 1, 3)
    return (attended, d_queries, d_neighbours)


def solution(mesh):
    n_seq, n_head = mesh.shape["seq"], mesh.shape["head"]
    block = NB_LEN // n_seq
    per_device = per_device_plain
    if n_head == 4 and block % 16 == 0:
        per_device = functools.partial(per_device_kernels, n_seq)
    in_specs = (
        P("seq", "head"),
        P(None, "seq", None, "head"),
        P(None, "head"),
        P(None, "head"),
        P("seq"),
        P("seq", None),
        P("seq", "head"),
    )
    out_specs = (P("seq", "head"), P("seq", "head"), P(None, "seq", None, "head"))
    return jax.shard_map(
        per_device, mesh=mesh, in_specs=in_specs, out_specs=out_specs, check_vma=False
    )
```
